32 devices in a mesh: feat: 8 (over y, x, core), batch: 4 (over z).
Axes of the slice: x: 2, y: 2, z: 4, core: 2. Of those that a mesh axis runs over, the one named last changes fastest.
Arguments:
- features: bfloat16 [32768, 4096], P('batch', 'feat'), may hold values from -6 to 6
- src_tile: int32 [32, 2], P('batch'), may hold values from 0 to 7
- rel_type: int32 [32, 2], P('batch'), may hold values from 0 to 3
- timestamps: int32 [4096], P(('batch', 'feat')), may hold values from 0 to 127
- edge_tiles: bfloat16 [4, 128, 1024], replicated, may hold values from -0.1875 to 0.1875
- rel_weight: bfloat16 [4, 4096, 512], P(None, 'feat'), may hold values from -0.09375 to 0.09375
- attn_gain: float32 [512], replicated, may hold values from 0.1 to 1.9
- w_qkv: bfloat16 [512, 1536], replicated, as said below
- w_out: bfloat16 [512, 512], replicated, may hold values from -0.25 to 0.25
- cotangent: bfloat16 [4096, 512], P(('batch', 'feat')), may hold values from -96 to 96
Outputs:
- layer_out: bfloat16 [4096, 512], P(('batch', 'feat'))
- grad_qkv: bfloat16 [512, 1536], replicated
- grad_out: bfloat16 [512, 512], replicated
- grad_gain: bfloat16 [512], replicated
- grad_rel: bfloat16 [4, 4096, 512], P(None, 'feat')
The draws below stay inside these ranges and needn't reach their ends.
Inputs may be any that keep to these rules, and one draw needn't show every extreme that they name: `src_tile`: index of a source tile within the batch group. `w_qkv`: query, key and value columns in that order along the second dimension.
All inputs are finite; a program needn't handle non-finite values.
Results may differ from the reference program's by a relative error of at most 0.014.
Values may be sent and summed in bfloat16 or wider, within the bound.
A program may use at most 128 MiB of HBM per device.

```python
import math
import jax
import jax.numpy as jnp
from jax import lax

F = 4096
D = 512
HEADS = 8
HEAD_DIM = 64
NREL = 4
SLOTS = 2
TBLK = 128
SBLK = 1024
SRC_BLOCKS = 8
ROWS_DEV = 128
ROWS = 1024
NBLK = 8
SRC = 8192
ALL_SRC = 32768
TOKENS = 4096
N_FEAT = 8
N_BATCH = 4


def draw_w_qkv(key, part):
    first = jax.random.fold_in(key, 0)
    whole = jax.random.normal(first, (D, 3 * D), jnp.float32) * D ** (-0.5)
    return whole.astype(jnp.bfloat16)


def draw_cotangent(key, part):
    first, second = jax.random.split(jax.random.fold_in(key, 71), 2)
    base = jnp.clip(jax.random.normal(first, (TOKENS, D), jnp.float32), -4.0, 4.0)
    sequences = TOKENS // ROWS_DEV
    owner = jax.random.permutation(second, D) % sequences
    row_sequence = jnp.arange(TOKENS, dtype=jnp.int32) // ROWS_DEV
    boost = jnp.where(row_sequence[:, None] == owner[None, :].astype(jnp.int32), 24.0, 1.0)
    return (base * boost).astype(jnp.bfloat16)


def with_ends(array, rng, smallest, top_value):
    shape = array.shape
    spot = [jax.random.randint(jax.random.fold_in(rng, axis), (), 0, shape[axis]) for axis in range(len(shape))]
    array = array.at[tuple(spot)].set(smallest)
    longest = shape.index(max(shape))
    spot[longest] = (spot[longest] + 1) % shape[longest]
    return array.at[tuple(spot)].set(top_value)


def steps_of(stream_key, shape, cuts, least, top_value):
    factor_of, own = 1.0, jax.random.fold_in(stream_key, 6)
    for axis_at, blocks in cuts:
        draws = jnp.exp(jax.random.uniform(jax.random.fold_in(own, axis_at), (blocks,), jnp.float32, least / len(cuts), top_value / len(cuts)))
        factor_of = factor_of * jnp.repeat(draws, shape[axis_at] // blocks).reshape([-1 if axis == axis_at else 1 for axis in range(len(shape))])
    return factor_of


def scatter_about(stream_key, dims, spread, most, shards=(), held_as=jnp.bfloat16):
    array = spread * jax.random.normal(stream_key, dims, jnp.float32)
    if shards:
        array = array * steps_of(stream_key, dims, shards, -0.22, 0.18)
    return jnp.clip(array, -most, most).astype(held_as)


def setup_inputs(seed: int = 0) -> dict:
    streams_of = jax.random.split(jax.random.key(seed), 11)
    return {
        "features": scatter_about(streams_of[0], (ALL_SRC, F), 1.0, 6.0, ((0, 4), (1, 8))),
        "src_tile": with_ends(jax.random.randint(streams_of[1], (N_BATCH * NBLK, SLOTS), 0, SRC_BLOCKS), jax.random.fold_in(streams_of[1], 1), 0, SRC_BLOCKS - 1).astype(jnp.int32),
        "rel_type": with_ends(jax.random.randint(streams_of[2], (N_BATCH * NBLK, SLOTS), 0, NREL), jax.random.fold_in(streams_of[2], 1), 0, NREL - 1).astype(jnp.int32),
        "timestamps": with_ends(jax.random.randint(streams_of[3], (TOKENS,), 0, ROWS_DEV), jax.random.fold_in(streams_of[3], 1), 0, ROWS_DEV - 1).astype(jnp.int32),
        "edge_tiles": scatter_about(streams_of[4], (NREL, TBLK, SBLK), SBLK ** -0.5, 0.1875),
        "rel_weight": scatter_about(streams_of[5], (NREL, F, D), F ** -0.5, 0.09375, ((1, 8),)),
        "attn_gain": jnp.clip(1.0 + 0.18 * jax.random.normal(streams_of[6], (D,), jnp.float32), 0.1, 1.9),
        "w_qkv": draw_w_qkv(jax.random.fold_in(streams_of[10], 71), 0),
        "w_out": scatter_about(streams_of[8], (D, D), D ** -0.5, 0.25),
        "cotangent": draw_cotangent(jax.random.fold_in(streams_of[10], 71), 0),
    }


EPS = 1e-06

def aggregate(feats, sources_all, kinds_all, edge_tiles):

    def one_block(pair):
        sources, kinds = pair
        parts = []
        for slot in range(SLOTS):
            piece = lax.dynamic_slice_in_dim(feats, (sources[slot] * SBLK).astype(jnp.int32), SBLK, 0)
            tile = lax.dynamic_index_in_dim(edge_tiles, kinds[slot].astype(jnp.int32), 0, keepdims=False)
            parts.append(jnp.dot(tile, piece, preferred_element_type=jnp.float32))
        member = (kinds[:, None] == jnp.arange(NREL, dtype=jnp.int32)[None, :]).astype(jnp.float32)
        merged = member[0][:, None, None] * parts[0][None]
        for slot in range(1, SLOTS):
            merged = merged + member[slot][:, None, None] * parts[slot][None]
        return merged.astype(jnp.bfloat16)
    blocks = lax.map(one_block, (sources_all, kinds_all))
    return jnp.moveaxis(blocks, 1, 0).reshape(NREL, -1, feats.shape[1])

def layer_forward(tokens, gain, w_qkv, w_out, times):
    token_values = tokens.astype(jnp.float32)
    scale = lax.rsqrt(lax.optimization_barrier(jnp.mean(token_values * token_values, axis=-1, keepdims=True)) + EPS)
    normed = (token_values * scale * gain).astype(jnp.bfloat16)
    projected = jnp.dot(normed, w_qkv, preferred_element_type=jnp.float32).astype(jnp.bfloat16)
    length = tokens.shape[0]
    queries = projected[:, :D].reshape(length, HEADS, HEAD_DIM).astype(jnp.float32)
    keys = projected[:, D:2 * D].reshape(length, HEADS, HEAD_DIM).astype(jnp.float32)
    contents = projected[:, 2 * D:].reshape(length, HEADS, HEAD_DIM).astype(jnp.float32)
    scores = jnp.einsum('qhd,khd->hqk', queries, keys) / math.sqrt(HEAD_DIM)
    allowed = times[None, :] <= times[:, None]
    scores = jnp.where(allowed[None], scores, -1e+30)
    weights = jax.nn.softmax(scores, axis=-1).astype(jnp.bfloat16)
    context = jnp.einsum('hqk,khd->qhd', weights.astype(jnp.float32), contents)
    context = context.astype(jnp.bfloat16).reshape(length, D)
    return (token_values + jnp.dot(context, w_out, preferred_element_type=jnp.float32)).astype(jnp.bfloat16)

def silu_slope(total):
    sigma = jax.nn.sigmoid(total)
    return sigma * (1.0 + total * (1.0 - sigma))

def reference(features, src_tile, rel_type, timestamps, edge_tiles, rel_weight, attn_gain, w_qkv, w_out, cotangent):
    groups = N_BATCH
    feats_all = features.reshape(groups, SRC, F)
    sources_all = src_tile.reshape(groups, NBLK, SLOTS)
    kinds_all = rel_type.reshape(groups, NBLK, SLOTS)
    times_all = timestamps.reshape(groups, N_FEAT, ROWS_DEV)
    cot_all = cotangent.reshape(groups, N_FEAT, ROWS_DEV, D)

    def group_step(carry, inputs):
        acc_qkv, acc_out, acc_gain, acc_rel = carry
        feats, sources, kinds, times, cots = inputs
        relations = aggregate(feats, sources, kinds, edge_tiles)
        total = jnp.dot(relations[0], rel_weight[0], preferred_element_type=jnp.float32)
        for relation in range(1, NREL):
            total = total + jnp.dot(relations[relation], rel_weight[relation], preferred_element_type=jnp.float32)
        hidden = jax.nn.silu(total).astype(jnp.bfloat16)
        sequences = hidden.reshape(N_FEAT, ROWS_DEV, D)

        def one_sequence(args):
            tokens, seq_times, seq_cot = args
            output, pullback = jax.vjp(lambda a, b, c, d: layer_forward(a, b, c, d, seq_times), tokens, attn_gain, w_qkv, w_out)
            return (output, pullback(seq_cot))
        outputs, grads = lax.map(one_sequence, (sequences, times, cots))
        d_tokens, d_gain, d_qkv, d_out = grads
        acc_qkv = acc_qkv + lax.optimization_barrier(jnp.sum(d_qkv.astype(jnp.float32), axis=0))
        acc_out = acc_out + lax.optimization_barrier(jnp.sum(d_out.astype(jnp.float32), axis=0))
        acc_gain = acc_gain + lax.optimization_barrier(jnp.sum(d_gain.astype(jnp.float32), axis=0))
        d_total = (d_tokens.reshape(ROWS, D).astype(jnp.float32) * silu_slope(total)).astype(jnp.bfloat16)
        rel_terms = jnp.stack([jnp.dot(relations[relation].T, d_total, preferred_element_type=jnp.float32) for relation in range(NREL)])
        acc_rel = acc_rel + rel_terms
        return ((acc_qkv, acc_out, acc_gain, acc_rel), outputs.reshape(ROWS, D))
    start = (jnp.zeros((D, 3 * D), jnp.float32), jnp.zeros((D, D), jnp.float32), jnp.zeros((D,), jnp.float32), jnp.zeros((NREL, F, D), jnp.float32))
    sums, outputs = lax.scan(group_step, start, (feats_all, sources_all, kinds_all, times_all, cot_all))
    layer_out = outputs.reshape(TOKENS, D)
    return (layer_out, sums[0].astype(jnp.bfloat16), sums[1].astype(jnp.bfloat16), sums[2].astype(jnp.bfloat16), sums[3].astype(jnp.bfloat16))
```

```python
import functools

import jax
import jax.numpy as jnp
from jax import lax
from jax.experimental import pallas as pl
from jax.experimental.pallas import tpu as pltpu
from jax.sharding import PartitionSpec as P

D = 512
HEADS = 8
HEAD_DIM = 64
NREL = 4
SLOTS = 2
SBLK = 1024
EPS = 1e-06
STEP = 128
LAG = 3
F32 = jnp.float32
BF16 = jnp.bfloat16
MESH = pl.DeviceIdType.MESH
NT = (((1,), (1,)), ((), ()))
TN = (((0,), (0,)), ((), ()))
NN = (((1,), (0,)), ((), ()))


def mm(a, b, dims=NN):
    return lax.dot_general(a, b, dims, preferred_element_type=F32)


def aggregate_kernel(src, kind, f0, f1, e0, e1, w, part, rel):
    b = pl.program_id(0)
    k0 = kind[SLOTS * b]
    k1 = kind[SLOTS * b + 1]
    p0 = mm(e0[0], f0[...])
    p1 = mm(e1[0], f1[...])
    same = k0 == k1
    first = jnp.where(same, p0 + p1, p0).astype(BF16)
    second = jnp.where(same, 0.0, p1).astype(BF16)
    rel[...] = jnp.zeros_like(rel)
    rel[k1] = second
    rel[k0] = first
    part[0, 0] = (mm(first, w[k0]) + mm(second, w[k1])).astype(BF16)


def aggregate(features, src_tile, rel_type, edge_tiles, rel_weight):
    blocks = src_tile.shape[0]
    tblk = edge_tiles.shape[1]
    cols = features.shape[1]

    def feature_block(slot):
        return pl.BlockSpec((SBLK, cols), lambda b, s, k: (s[SLOTS * b + slot], 0))

    def edge_block(slot):
        return pl.BlockSpec((1, tblk, SBLK), lambda b, s, k: (k[SLOTS * b + slot], 0, 0))

    return pl.pallas_call(
        aggregate_kernel,
        grid_spec=pltpu.PrefetchScalarGridSpec(
            num_scalar_prefetch=2,
            grid=(blocks,),
            in_specs=[
                feature_block(0),
                feature_block(1),
                edge_block(0),
                edge_block(1),
                pl.BlockSpec((NREL, cols, D), lambda b, s, k: (0, 0, 0)),
            ],
            out_specs=[
                pl.BlockSpec((1, 1, tblk, D), lambda b, s, k: (b % 2, b // 2, 0, 0)),
                pl.BlockSpec((NREL, tblk, cols), lambda b, s, k: (0, b, 0)),
            ],
        ),
        out_shape=[
            jax.ShapeDtypeStruct((2, blocks // 2, tblk, D), BF16),
            jax.ShapeDtypeStruct((NREL, blocks * tblk, cols), BF16),
        ],
        compiler_params=pltpu.CompilerParams(vmem_limit_bytes=40 * 2**20),
        name="aggregate",
    )(src_tile.reshape(-1), rel_type.reshape(-1), features, features, edge_tiles, edge_tiles, rel_weight)


def remote(src, dst, send, recv, device):
    return pltpu.make_async_remote_copy(
        src_ref=src, dst_ref=dst, send_sem=send, recv_sem=recv, device_id=device, device_id_type=MESH
    )


def step_kernel(
    nf, nb, part, rel, trow, tcol, gain, wqkv, wout, cot,
    out, grads, gain_out, grel,
    rs_sib, rs_stage, rs_recv, dt, gterm, g_sib, g_stage, g_recv,
    zl, zr, zs, gzl, gzr, gzs, gain_in, gain_z, proj, ctx, dproj,
    rs_s, rs_r, g_s, g_r, dt_s, dt_r, ag_s, ag_r, ga_s, ga_r, gz_s, gz_r,
    red_s, redl_r, redr_r, bl_s, br_s, bc_r,
):
    me = lax.axis_index("feat")
    z = lax.axis_index("batch")
    nc = nf // 2
    chip, core = me // 2, me % 2
    sib = me + 1 - 2 * core
    sibling = {"feat": sib}
    rows, cols = rel.shape[1], rel.shape[2]
    quarters = cols // STEP
    chunks = NREL * quarters
    length = out.shape[0]
    slab = D // nf

    def ahead(d):
        return 2 * ((chip + d) % nc) + core

    def behind(d):
        return 2 * ((chip + nc - d) % nc) + core

    barrier = pltpu.get_barrier_semaphore()
    pl.semaphore_signal(barrier, inc=1, device_id=sibling, device_id_type=MESH)
    for d in range(1, nc):
        pl.semaphore_signal(barrier, inc=1, device_id={"feat": ahead(d)}, device_id_type=MESH)
    for d in range(1, nb):
        pl.semaphore_signal(barrier, inc=1, device_id={"batch": (z + d) % nb}, device_id_type=MESH)
    pl.semaphore_wait(barrier, nc + nb - 1)

    def rs_pair(src, half, send, recv):
        return remote(src.at[1 - core], half, send.at[0], recv.at[0], sibling)

    def rs_chip(stage, landed, send, recv, d):
        return remote(stage.at[(chip + d) % nc], landed.at[d], send.at[d], recv.at[d], {"feat": ahead(d)})

    def rs_mid(src, half, stage, landed, send, recv):
        rs_pair(src, half, send, recv).wait_recv()
        for d in range(1, nc):
            c = (chip + d) % nc
            stage[c] = (src[core, c].astype(F32) + half[c].astype(F32)).astype(BF16)
            rs_chip(stage, landed, send, recv, d).start()

    def rs_end(src, half, stage, landed, send, recv):
        value = src[core, chip].astype(F32) + half[chip].astype(F32)
        for d in range(1, nc):
            rs_chip(stage, landed, send, recv, d).wait_recv()
            value = value + landed[d].astype(F32)
        return value

    def rs_drain(src, half, stage, landed, send, recv):
        rs_pair(src, half, send, recv).wait_send()
        for d in range(1, nc):
            rs_chip(stage, landed, send, recv, d).wait_send()

    def ag_copy(buf, send, recv, d):
        device = sibling if d == 0 else {"feat": ahead(d)}
        return remote(buf.at[me], buf.at[me], send.at[d], recv.at[d], device)

    def ag_hand(buf, send, recv, d):
        slot = behind(d)
        return remote(buf.at[slot], buf.at[slot], send.at[nc - 1 + d], recv.at[nc - 1 + d], sibling)

    def ag_landed(buf, send, recv, slot, index):
        return remote(buf.at[slot], buf.at[slot], send.at[index], recv.at[index], sibling)

    def ag_start(*group):
        for d in list(range(1, nc)) + [0]:
            ag_copy(*group, d).start()

    def ag_mid(*group):
        for d in range(1, nc):
            ag_landed(*group, behind(d), d).wait_recv()
            ag_hand(*group, d).start()

    def ag_end(*group):
        ag_landed(*group, sib, 0).wait_recv()
        for d in range(1, nc):
            ag_landed(*group, behind(d) + 1 - 2 * core, nc - 1 + d).wait_recv()

    def ag_drain(*group):
        for d in range(nc):
            ag_copy(*group, d).wait_send()
        for d in range(1, nc):
            ag_hand(*group, d).wait_send()

    total_rs = (part, rs_sib, rs_stage, rs_recv, rs_s, rs_r)
    grad_rs = (gterm, g_sib, g_stage, g_recv, g_s, g_r)
    dt_ag = (dt, dt_s, dt_r)
    grad_ag = (grads, ag_s, ag_r)
    gain_ag = (gain_in, ga_s, ga_r)

    rs_pair(part, rs_sib, rs_s, rs_r).start()
    rs_mid(*total_rs)
    total = rs_end(*total_rs)

    sigma = 1.0 / (1.0 + jnp.exp(-total))
    tokens = (total * sigma).astype(BF16).astype(F32)
    scale = lax.rsqrt(jnp.mean(tokens * tokens, axis=-1, keepdims=True) + EPS)
    normed = (tokens * scale * gain[...]).astype(BF16)
    proj[...] = mm(normed, wqkv[...]).astype(BF16)
    allowed = trow[...] <= tcol[...]
    d_ctx = mm(cot[...], wout[...], NT).astype(BF16)
    for h in range(HEADS):
        a, b = h * HEAD_DIM, (h + 1) * HEAD_DIM
        q = proj[:, a:b]
        k = proj[:, D + a : D + b]
        v = proj[:, 2 * D + a : 2 * D + b]
        scores = jnp.where(allowed, mm(q, k, NT) * (HEAD_DIM**-0.5), -1e30)
        e = jnp.exp(scores - jnp.max(scores, axis=-1, keepdims=True))
        p = e / jnp.sum(e, axis=-1, keepdims=True)
        weights = p.astype(BF16)
        ctx[:, a:b] = mm(weights, v).astype(BF16)
        dc = d_ctx[:, a:b]
        dproj[:, 2 * D + a : 2 * D + b] = mm(weights, dc, TN).astype(BF16)
        dw = mm(dc, v, NT).astype(BF16).astype(F32)
        ds = p * (dw - jnp.sum(dw * p, axis=-1, keepdims=True))
        ds = (jnp.where(allowed, ds, 0.0) * (HEAD_DIM**-0.5)).astype(BF16)
        dproj[:, a:b] = mm(ds, k).astype(BF16)
        dproj[:, D + a : D + b] = mm(ds, q, TN).astype(BF16)
    d_normed = mm(dproj[...], wqkv[...], NT).astype(BF16).astype(F32)
    u = d_normed * gain[...]
    inner = jnp.sum(u * tokens, axis=-1, keepdims=True)
    d_tokens = cot[...].astype(F32) + u * scale - tokens * (scale * scale * scale * inner * (1.0 / D))
    d_hidden = d_tokens.astype(BF16).astype(F32)
    dt[me] = (d_hidden * (sigma * (1.0 + total * (1.0 - sigma)))).astype(BF16)
    ag_start(*dt_ag)
    gain_term = jnp.sum(d_normed * (tokens * scale), axis=0, keepdims=True)
    gain_in[me] = jnp.broadcast_to(gain_term, (8, D))
    out[...] = (tokens + mm(ctx[...], wout[...])).astype(BF16)
    g_qkv = mm(normed, dproj[...], TN).astype(BF16)
    for j in range(nf):
        gterm[j % 2, j // 2, :, : 3 * D] = g_qkv[j * slab : (j + 1) * slab]
    g_out = mm(ctx[...], cot[...], TN).astype(BF16)
    for j in range(nf):
        gterm[j % 2, j // 2, :, 3 * D :] = g_out[j * slab : (j + 1) * slab]
    rs_pair(gterm, g_sib, g_s, g_r).start()
    ag_start(*gain_ag)
    ag_mid(*dt_ag)
    rs_mid(*grad_rs)
    ag_end(*dt_ag)

    owner = nb // 2 - 1 + core
    up, down = {"batch": lax.rem(z + 1, nb)}, {"batch": lax.rem(z + nb - 1, nb)}

    def hop_up(stage, landed, i):
        return remote(stage, landed, red_s.at[i], redl_r.at[i], up)

    def hop_down(stage, landed, i):
        return remote(stage, landed, red_s.at[i], redr_r.at[i], down)

    def give_up(result, i):
        return remote(result, result, br_s.at[i], bc_r.at[i], up)

    def give_down(result, i):
        return remote(result, result, bl_s.at[i], bc_r.at[i], down)

    def reduce(own, low, high, stage, result, i):
        @pl.when(z == 0)
        def _():
            stage[...] = own.astype(BF16)
            hop_up(stage, low, i).start()

        @pl.when((z > 0) & (z < owner))
        def _():
            hop_up(stage, low, i).wait_recv()
            stage[...] = (own + low[...].astype(F32)).astype(BF16)
            hop_up(stage, low, i).start()

        @pl.when(z == nb - 1)
        def _():
            stage[...] = own.astype(BF16)
            hop_down(stage, high, i).start()

        @pl.when((z > owner) & (z < nb - 1))
        def _():
            hop_down(stage, high, i).wait_recv()
            stage[...] = (own + high[...].astype(F32)).astype(BF16)
            hop_down(stage, high, i).start()

        @pl.when(z == owner)
        def _():
            hop_up(stage, low, i).wait_recv()
            hop_down(stage, high, i).wait_recv()
            result[...] = (own + low[...].astype(F32) + high[...].astype(F32)).astype(BF16)
            give_up(result, i).start()
            give_down(result, i).start()

    def spread(result, i):
        @pl.when(z != owner)
        def _():
            give_up(result, i).wait_recv()

        @pl.when((z < owner) & (z > 0))
        def _():
            give_down(result, i).start()

        @pl.when((z > owner) & (z < nb - 1))
        def _():
            give_up(result, i).start()

    def drain(low, stage, result, i):
        @pl.when(z != owner)
        def _():
            hop_up(stage, low, i).wait_send()

        @pl.when((z <= owner) & (z > 0))
        def _():
            give_down(result, i).wait_send()

        @pl.when((z >= owner) & (z < nb - 1))
        def _():
            give_up(result, i).wait_send()

    def chunk_out(i):
        return grel.at[pl.ds(pl.multiple_of(i * STEP, STEP), STEP)]

    def reduce_rel(i):
        left = rel[i // quarters, :, pl.ds(pl.multiple_of((i % quarters) * STEP, STEP), STEP)]
        own = mm(left, dt[...].reshape(rows, D), TN)
        reduce(own, zl.at[i], zr.at[i], zs.at[i], chunk_out(i), i)

    def both(i, carry):
        reduce_rel(i)
        spread(chunk_out(i - LAG), i - LAG)
        return carry

    def only_reduce(i, carry):
        reduce_rel(i)
        return carry

    def only_spread(i, carry):
        spread(chunk_out(i), i)
        return carry

    turn = max(LAG, chunks // 4)
    mine = grads.at[me]
    lax.fori_loop(0, LAG, only_reduce, 0)
    lax.fori_loop(LAG, turn, both, 0)
    ag_mid(*gain_ag)
    ag_end(*gain_ag)
    group_gain = gain_in[0]
    for j in range(1, nf):
        group_gain = group_gain + gain_in[j]
    gain_z[z] = group_gain

    def gain_copy(d):
        return remote(gain_z.at[z], gain_z.at[z], gz_s.at[d], gz_r.at[d], {"batch": (z + d) % nb})

    def gain_landed(d):
        slot = (z + nb - d) % nb
        return remote(gain_z.at[slot], gain_z.at[slot], gz_s.at[d], gz_r.at[d], {"batch": slot})

    for d in range(1, nb):
        gain_copy(d).start()
    reduce(rs_end(*grad_rs), gzl, gzr, gzs, mine, chunks)
    lax.fori_loop(turn, turn + LAG, both, 0)
    spread(mine, chunks)
    ag_start(*grad_ag)
    lax.fori_loop(turn + LAG, chunks, both, 0)
    ag_mid(*grad_ag)
    lax.fori_loop(chunks - LAG, chunks, only_spread, 0)
    for d in range(1, nb):
        gain_landed(d).wait_recv()
    whole_gain = gain_z[0]
    for j in range(1, nb):
        whole_gain = whole_gain + gain_z[j]
    gain_out[...] = whole_gain
    ag_end(*grad_ag)

    def drain_rel(i, carry):
        drain(zl.at[i], zs.at[i], chunk_out(i), i)
        return carry

    lax.fori_loop(0, chunks, drain_rel, 0)
    drain(gzl, gzs, mine, chunks)
    for d in range(1, nb):
        gain_copy(d).wait_send()
    rs_drain(*total_rs)
    rs_drain(*grad_rs)
    ag_drain(*dt_ag)
    ag_drain(*gain_ag)
    ag_drain(*grad_ag)


def training_step(nf, nb, part, rel, timestamps, gain, w_qkv, w_out, cotangent):
    nc = nf // 2
    length = timestamps.shape[0]
    cols = rel.shape[2]
    slab = D // nf
    chunks = NREL * cols // STEP
    vmem = pl.BlockSpec(memory_space=pltpu.VMEM)
    blocks = pltpu.VMEM((nc, length, D), BF16)
    slabs = pltpu.VMEM((nc, slab, 4 * D), BF16)
    pieces = pltpu.VMEM((chunks, STEP, D), BF16)
    piece = pltpu.VMEM((slab, 4 * D), BF16)
    dma = pltpu.SemaphoreType.DMA
    return pl.pallas_call(
        functools.partial(step_kernel, nf, nb),
        out_shape=[
            jax.ShapeDtypeStruct((length, D), BF16),
            jax.ShapeDtypeStruct((nf, slab, 4 * D), BF16),
            jax.ShapeDtypeStruct((8, D), F32),
            jax.ShapeDtypeStruct((NREL * cols, D), BF16),
        ],
        in_specs=[vmem] * 8,
        out_specs=[vmem] * 4,
        scratch_shapes=[
            blocks, blocks, blocks,
            pltpu.VMEM((nf, length, D), BF16),
            pltpu.VMEM((2, nc, slab, 4 * D), BF16),
            slabs, slabs, slabs,
            pieces, pieces, pieces,
            piece, piece, piece,
            pltpu.VMEM((nf, 8, D), F32),
            pltpu.VMEM((nb, 8, D), F32),
            pltpu.VMEM((length, 3 * D), BF16),
            pltpu.VMEM((length, D), BF16),
            pltpu.VMEM((length, 3 * D), BF16),
        ]
        + [dma((nc,))] * 4
        + [dma((2 * nc - 1,))] * 6
        + [dma((nb,))] * 2
        + [dma((chunks + 1,))] * 6,
        compiler_params=pltpu.CompilerParams(
            collective_id=0, has_side_effects=True, vmem_limit_bytes=52 * 2**20
        ),
        name="training_step",
    )(part, rel, timestamps.reshape(1, -1), timestamps.reshape(-1, 1), gain.reshape(1, -1), w_qkv, w_out, cotangent)


def solution(mesh):
    nf, nb = mesh.shape["feat"], mesh.shape["batch"]

    def shards(
        features, src_tile, rel_type, timestamps, edge_tiles,
        rel_weight, attn_gain, w_qkv, w_out, cotangent,
    ):
        part, rel = aggregate(features, src_tile, rel_type, edge_tiles, rel_weight)
        layer_out, grads, gain, grel = training_step(
            nf, nb, part, rel, timestamps, attn_gain, w_qkv, w_out, cotangent
        )
        grads = grads.reshape(D, 4 * D)
        return (
            layer_out,
            grads[:, : 3 * D],
            grads[:, 3 * D :],
            gain[0].astype(BF16),
            grel.reshape(NREL, rel.shape[2], D),
        )

    in_specs = (
        P("batch", "feat"),
        P("batch", None),
        P("batch", None),
        P(("batch", "feat")),
        P(),
        P(None, "feat", None),
        P(),
        P(),
        P(),
        P(("batch", "feat"), None),
    )
    out_specs = (P(("batch", "feat"), None), P(), P(), P(), P(None, "feat", None))
    return jax.shard_map(shards, mesh=mesh, in_specs=in_specs, out_specs=out_specs, check_vma=False)
```

```python
import functools

import jax
import jax.numpy as jnp
from jax import lax
from jax.experimental import pallas as pl
from jax.experimental.pallas import tpu as pltpu
from jax.sharding import PartitionSpec as P

D = 512
HEADS = 8
HEAD_DIM = 64
NREL = 4
SLOTS = 2
SBLK = 1024
EPS = 1e-06
STEP = 128
LAG = 6
F32 = jnp.float32
BF16 = jnp.bfloat16
MESH = pl.DeviceIdType.MESH
NT = (((1,), (1,)), ((), ()))
TN = (((0,), (0,)), ((), ()))
NN = (((1,), (0,)), ((), ()))


def mm(a, b, dims=NN):
    return lax.dot_general(a, b, dims, preferred_element_type=F32)


def aggregate_kernel(src, kind, f0, f1, e0, e1, w, part, rel):
    b = pl.program_id(0)
    k0 = kind[0, b]
    k1 = kind[1, b]
    p0 = mm(e0[0], f0[...])
    p1 = mm(e1[0], f1[...])
    same = k0 == k1
    first = jnp.where(same, p0 + p1, p0).astype(BF16)
    second = jnp.where(same, 0.0, p1).astype(BF16)
    rel[...] = jnp.zeros_like(rel)
    rel[k1] = second
    rel[k0] = first
    part[0, 0] = (mm(first, w[k0]) + mm(second, w[k1])).astype(BF16)


def aggregate(features, src_tile, rel_type, edge_tiles, rel_weight):
    blocks = src_tile.shape[0]
    tblk = edge_tiles.shape[1]
    cols = features.shape[1]

    def feature_block(slot):
        return pl.BlockSpec((SBLK, cols), lambda b, s, k: (s[slot, b], 0))

    def edge_block(slot):
        return pl.BlockSpec((1, tblk, SBLK), lambda b, s, k: (k[slot, b], 0, 0))

    return pl.pallas_call(
        aggregate_kernel,
        grid_spec=pltpu.PrefetchScalarGridSpec(
            num_scalar_prefetch=2,
            grid=(blocks,),
            in_specs=[
                feature_block(0),
                feature_block(1),
                edge_block(0),
                edge_block(1),
                pl.BlockSpec((NREL, cols, D), lambda b, s, k: (0, 0, 0)),
            ],
            out_specs=[
                pl.BlockSpec((1, 1, tblk, D), lambda b, s, k: (b % 2, b // 2, 0, 0)),
                pl.BlockSpec((NREL, tblk, cols), lambda b, s, k: (0, b, 0)),
            ],
        ),
        out_shape=[
            jax.ShapeDtypeStruct((2, blocks // 2, tblk, D), BF16),
            jax.ShapeDtypeStruct((NREL, blocks * tblk, cols), BF16),
        ],
        compiler_params=pltpu.CompilerParams(vmem_limit_bytes=60 * 2**20),
        name="aggregate",
    )(src_tile.T, rel_type.T, features, features, edge_tiles, edge_tiles, rel_weight)


def remote(src, dst, send, recv, device):
    return pltpu.make_async_remote_copy(
        src_ref=src, dst_ref=dst, send_sem=send, recv_sem=recv, device_id=device, device_id_type=MESH
    )


def step_kernel(
    nf, nb, part, rel, times, gain, wqkv, wout, cot,
    out, qkv_out, w_out_out, gain_out, grel,
    grads, rs_sib, rs_stage, rs_recv, dt, gterm, g_sib, g_stage, g_recv,
    zl, zr, zs, gzl, gzr, gzs, gain_in, gain_z, proj, ctx, dproj,
    rs_s, rs_r, g_s, g_r, dt_s, dt_r, ag_s, ag_r, ga_s, ga_r, gz_s, gz_r,
    red_s, redl_r, redr_r, bl_s, br_s, bc_r,
):
    me = lax.axis_index("feat")
    z = lax.axis_index("batch")
    nc = nf // 2
    chip, core = me // 2, me % 2
    sib = me + 1 - 2 * core
    sibling = {"feat": sib}
    rows, cols = rel.shape[1], rel.shape[2]
    quarters = cols // STEP
    chunks = NREL * quarters
    length = out.shape[0]
    slab = D // nf

    def ahead(d):
        return 2 * ((chip + d) % nc) + core

    def behind(d):
        return 2 * ((chip + nc - d) % nc) + core

    barrier = pltpu.get_barrier_semaphore()
    pl.semaphore_signal(barrier, inc=1, device_id=sibling, device_id_type=MESH)
    for d in range(1, nc):
        pl.semaphore_signal(barrier, inc=1, device_id={"feat": ahead(d)}, device_id_type=MESH)
    for d in range(1, nb):
        pl.semaphore_signal(barrier, inc=1, device_id={"batch": (z + d) % nb}, device_id_type=MESH)
    pl.semaphore_wait(barrier, nc + nb - 1)

    def rs_pair(src, half, send, recv):
        return remote(src.at[1 - core], half, send.at[0], recv.at[0], sibling)

    def rs_chip(stage, landed, send, recv, d):
        return remote(stage.at[(chip + d) % nc], landed.at[d], send.at[d], recv.at[d], {"feat": ahead(d)})

    def rs_mid(src, half, stage, landed, send, recv):
        rs_pair(src, half, send, recv).wait_recv()
        for d in range(1, nc):
            c = (chip + d) % nc
            stage[c] = (src[core, c].astype(F32) + half[c].astype(F32)).astype(BF16)
            rs_chip(stage, landed, send, recv, d).start()

    def rs_end(src, half, stage, landed, send, recv):
        value = src[core, chip].astype(F32) + half[chip].astype(F32)
        for d in range(1, nc):
            rs_chip(stage, landed, send, recv, d).wait_recv()
            value = value + landed[d].astype(F32)
        return value

    def rs_drain(src, half, stage, landed, send, recv):
        rs_pair(src, half, send, recv).wait_send()
        for d in range(1, nc):
            rs_chip(stage, landed, send, recv, d).wait_send()

    def ag_copy(buf, send, recv, d):
        device = sibling if d == 0 else {"feat": ahead(d)}
        return remote(buf.at[me], buf.at[me], send.at[d], recv.at[d], device)

    def ag_hand(buf, send, recv, d):
        slot = behind(d)
        return remote(buf.at[slot], buf.at[slot], send.at[nc - 1 + d], recv.at[nc - 1 + d], sibling)

    def ag_landed(buf, send, recv, slot, index):
        return remote(buf.at[slot], buf.at[slot], send.at[index], recv.at[index], sibling)

    def ag_start(*group):
        for d in list(range(1, nc)) + [0]:
            ag_copy(*group, d).start()

    def ag_mid(*group):
        for d in range(1, nc):
            ag_landed(*group, behind(d), d).wait_recv()
            ag_hand(*group, d).start()

    def ag_end(*group):
        ag_landed(*group, sib, 0).wait_recv()
        for d in range(1, nc):
            ag_landed(*group, behind(d) + 1 - 2 * core, nc - 1 + d).wait_recv()

    def ag_drain(*group):
        for d in range(nc):
            ag_copy(*group, d).wait_send()
        for d in range(1, nc):
            ag_hand(*group, d).wait_send()

    total_rs = (part, rs_sib, rs_stage, rs_recv, rs_s, rs_r)
    grad_rs = (gterm, g_sib, g_stage, g_recv, g_s, g_r)
    dt_ag = (dt, dt_s, dt_r)
    grad_ag = (grads, ag_s, ag_r)
    gain_ag = (gain_in, ga_s, ga_r)

    rs_pair(part, rs_sib, rs_s, rs_r).start()
    d_ctx = mm(cot[...], wout[...], NT).astype(BF16)
    row_times = jnp.broadcast_to(times[...], (length, length))
    allowed = row_times <= row_times.T
    rs_mid(*total_rs)
    total = rs_end(*total_rs)

    sigma = 1.0 / (1.0 + jnp.exp(-total))
    tokens = (total * sigma).astype(BF16).astype(F32)
    scale = lax.rsqrt(jnp.mean(tokens * tokens, axis=-1, keepdims=True) + EPS)
    normed = (tokens * scale * gain[...]).astype(BF16)
    proj[...] = mm(normed, wqkv[...]).astype(BF16)
    heads = range(HEADS)
    spans = [(h * HEAD_DIM, (h + 1) * HEAD_DIM) for h in heads]
    q = [proj[:, a:b] for a, b in spans]
    k = [proj[:, D + a : D + b] for a, b in spans]
    v = [proj[:, 2 * D + a : 2 * D + b] for a, b in spans]
    dc = [d_ctx[:, a:b] for a, b in spans]
    scores = [mm(q[h], k[h], NT) for h in heads]
    dw = [mm(dc[h], v[h], NT) for h in heads]
    p, ds = [], []
    for h in heads:
        masked = jnp.where(allowed, scores[h] * (HEAD_DIM**-0.5), -1e30)
        e = jnp.exp(masked - jnp.max(masked, axis=-1, keepdims=True))
        ph = e / jnp.sum(e, axis=-1, keepdims=True)
        dwh = dw[h].astype(BF16).astype(F32)
        dsh = ph * (dwh - jnp.sum(dwh * ph, axis=-1, keepdims=True))
        p.append(ph.astype(BF16))
        ds.append((jnp.where(allowed, dsh, 0.0) * (HEAD_DIM**-0.5)).astype(BF16))
    for h, (a, b) in enumerate(spans):
        dproj[:, a:b] = mm(ds[h], k[h]).astype(BF16)
        dproj[:, D + a : D + b] = mm(ds[h], q[h], TN).astype(BF16)
        dproj[:, 2 * D + a : 2 * D + b] = mm(p[h], dc[h], TN).astype(BF16)
    d_normed = mm(dproj[...], wqkv[...], NT).astype(BF16).astype(F32)
    u = d_normed * gain[...]
    inner = jnp.sum(u * tokens, axis=-1, keepdims=True)
    d_tokens = cot[...].astype(F32) + u * scale - tokens * (scale * scale * scale * inner * (1.0 / D))
    d_hidden = d_tokens.astype(BF16).astype(F32)
    dt[me] = (d_hidden * (sigma * (1.0 + total * (1.0 - sigma)))).astype(BF16)
    ag_start(*dt_ag)
    gain_term = jnp.sum(d_normed * (tokens * scale), axis=0, keepdims=True)
    gain_in[me] = jnp.broadcast_to(gain_term, (8, D))
    for h, (a, b) in enumerate(spans):
        ctx[:, a:b] = mm(p[h], v[h]).astype(BF16)
    out[...] = (tokens + mm(ctx[...], wout[...])).astype(BF16)
    g_qkv = mm(normed, dproj[...], TN).astype(BF16)
    for j in range(nf):
        gterm[j % 2, j // 2, :, : 3 * D] = g_qkv[j * slab : (j + 1) * slab]
    g_out = mm(ctx[...], cot[...], TN).astype(BF16)
    for j in range(nf):
        gterm[j % 2, j // 2, :, 3 * D :] = g_out[j * slab : (j + 1) * slab]
    rs_pair(gterm, g_sib, g_s, g_r).start()
    ag_start(*gain_ag)
    ag_mid(*dt_ag)
    rs_mid(*grad_rs)
    ag_end(*dt_ag)

    owner = nb // 2 - 1 + core
    up, down = {"batch": lax.rem(z + 1, nb)}, {"batch": lax.rem(z + nb - 1, nb)}

    def hop_up(stage, landed, i):
        return remote(stage, landed, red_s.at[i], redl_r.at[i], up)

    def hop_down(stage, landed, i):
        return remote(stage, landed, red_s.at[i], redr_r.at[i], down)

    def give_up(result, i):
        return remote(result, result, br_s.at[i], bc_r.at[i], up)

    def give_down(result, i):
        return remote(result, result, bl_s.at[i], bc_r.at[i], down)

    def reduce(own, low, high, stage, result, i):
        @pl.when(z == 0)
        def _():
            stage[...] = own.astype(BF16)
            hop_up(stage, low, i).start()

        @pl.when((z > 0) & (z < owner))
        def _():
            hop_up(stage, low, i).wait_recv()
            stage[...] = (own + low[...].astype(F32)).astype(BF16)
            hop_up(stage, low, i).start()

        @pl.when(z == nb - 1)
        def _():
            stage[...] = own.astype(BF16)
            hop_down(stage, high, i).start()

        @pl.when((z > owner) & (z < nb - 1))
        def _():
            hop_down(stage, high, i).wait_recv()
            stage[...] = (own + high[...].astype(F32)).astype(BF16)
            hop_down(stage, high, i).start()

        @pl.when(z == owner)
        def _():
            hop_up(stage, low, i).wait_recv()
            hop_down(stage, high, i).wait_recv()
            result[...] = (own + low[...].astype(F32) + high[...].astype(F32)).astype(BF16)
            give_up(result, i).start()
            give_down(result, i).start()

    edge = (z == 0) | (z == nb - 1)

    def spread(result, i):
        @pl.when((z > 0) & (z < owner))
        def _():
            give_down(result, i).wait_recv()
            give_down(result, i).start()

        @pl.when((z > owner) & (z < nb - 1))
        def _():
            give_up(result, i).wait_recv()
            give_up(result, i).start()

    def settle(result, i):
        @pl.when(edge)
        def _():
            give_up(result, i).wait_recv()

    def drain(low, stage, result, i):
        @pl.when(z != owner)
        def _():
            hop_up(stage, low, i).wait_send()

        @pl.when((z <= owner) & (z > 0))
        def _():
            give_down(result, i).wait_send()

        @pl.when((z >= owner) & (z < nb - 1))
        def _():
            give_up(result, i).wait_send()

    def chunk_out(i):
        return grel.at[pl.ds(pl.multiple_of(i * STEP, STEP), STEP)]

    def reduce_rel(i):
        left = rel[i // quarters, :, pl.ds(pl.multiple_of((i % quarters) * STEP, STEP), STEP)]
        own = mm(left, dt[...].reshape(rows, D), TN)
        reduce(own, zl.at[i], zr.at[i], zs.at[i], chunk_out(i), i)

    def both(i, carry):
        reduce_rel(i)
        spread(chunk_out(i - lag), i - lag)
        return carry

    def only_reduce(i, carry):
        reduce_rel(i)
        return carry

    def only_spread(i, carry):
        spread(chunk_out(i), i)
        return carry

    def only_settle(i, carry):
        settle(chunk_out(i), i)
        return carry

    lag = min(LAG, chunks // 2)
    turn = lag
    mine = grads.at[me]
    lax.fori_loop(0, lag, only_reduce, 0)
    ag_mid(*gain_ag)
    ag_end(*gain_ag)
    group_gain = gain_in[0]
    for j in range(1, nf):
        group_gain = group_gain + gain_in[j]
    gain_z[z] = group_gain

    def gain_copy(d):
        return remote(gain_z.at[z], gain_z.at[z], gz_s.at[d], gz_r.at[d], {"batch": (z + d) % nb})

    def gain_landed(d):
        slot = (z + nb - d) % nb
        return remote(gain_z.at[slot], gain_z.at[slot], gz_s.at[d], gz_r.at[d], {"batch": slot})

    for d in range(1, nb):
        gain_copy(d).start()
    reduce(rs_end(*grad_rs), gzl, gzr, gzs, mine, chunks)
    lax.fori_loop(turn, turn + lag, both, 0)
    spread(mine, chunks)

    @pl.when(jnp.logical_not(edge))
    def _():
        ag_start(*grad_ag)

    lax.fori_loop(turn + lag, chunks, both, 0)
    settle(mine, chunks)

    @pl.when(edge)
    def _():
        ag_start(*grad_ag)

    ag_mid(*grad_ag)
    lax.fori_loop(chunks - lag, chunks, only_spread, 0)
    lax.fori_loop(0, chunks, only_settle, 0)
    for d in range(1, nb):
        gain_landed(d).wait_recv()
    whole_gain = gain_z[0]
    for j in range(1, nb):
        whole_gain = whole_gain + gain_z[j]
    gain_out[...] = whole_gain
    ag_end(*grad_ag)
    for j in range(nf):
        qkv_out[j * slab : (j + 1) * slab] = grads[j, :, : 3 * D]
        w_out_out[j * slab : (j + 1) * slab] = grads[j, :, 3 * D :]

    def drain_rel(i, carry):
        drain(zl.at[i], zs.at[i], chunk_out(i), i)
        return carry

    lax.fori_loop(0, chunks, drain_rel, 0)
    drain(gzl, gzs, mine, chunks)
    for d in range(1, nb):
        gain_copy(d).wait_send()
    rs_drain(*total_rs)
    rs_drain(*grad_rs)
    ag_drain(*dt_ag)
    ag_drain(*gain_ag)
    ag_drain(*grad_ag)


def training_step(nf, nb, part, rel, timestamps, gain, w_qkv, w_out, cotangent):
    nc = nf // 2
    length = timestamps.shape[0]
    cols = rel.shape[2]
    slab = D // nf
    chunks = NREL * cols // STEP
    vmem = pl.BlockSpec(memory_space=pltpu.VMEM)
    blocks = pltpu.VMEM((nc, length, D), BF16)
    slabs = pltpu.VMEM((nc, slab, 4 * D), BF16)
    pieces = pltpu.VMEM((chunks, STEP, D), BF16)
    piece = pltpu.VMEM((slab, 4 * D), BF16)
    dma = pltpu.SemaphoreType.DMA
    return pl.pallas_call(
        functools.partial(step_kernel, nf, nb),
        out_shape=[
            jax.ShapeDtypeStruct((length, D), BF16),
            jax.ShapeDtypeStruct((D, 3 * D), BF16),
            jax.ShapeDtypeStruct((D, D), BF16),
            jax.ShapeDtypeStruct((8, D), F32),
            jax.ShapeDtypeStruct((NREL * cols, D), BF16),
        ],
        in_specs=[vmem] * 7,
        out_specs=[vmem] * 5,
        scratch_shapes=[
            pltpu.VMEM((nf, slab, 4 * D), BF16),
            blocks, blocks, blocks,
            pltpu.VMEM((nf, length, D), BF16),
            pltpu.VMEM((2, nc, slab, 4 * D), BF16),
            slabs, slabs, slabs,
            pieces, pieces, pieces,
            piece, piece, piece,
            pltpu.VMEM((nf, 8, D), F32),
            pltpu.VMEM((nb, 8, D), F32),
            pltpu.VMEM((length, 3 * D), BF16),
            pltpu.VMEM((length, D), BF16),
            pltpu.VMEM((length, 3 * D), BF16),
        ]
        + [dma((nc,))] * 4
        + [dma((2 * nc - 1,))] * 6
        + [dma((nb,))] * 2
        + [dma((chunks + 1,))] * 6,
        compiler_params=pltpu.CompilerParams(
            collective_id=0, has_side_effects=True, vmem_limit_bytes=60 * 2**20
        ),
        name="training_step",
    )(part, rel, timestamps.reshape(1, -1), gain.reshape(1, -1), w_qkv, w_out, cotangent)


def solution(mesh):
    nf, nb = mesh.shape["feat"], mesh.shape["batch"]

    def shards(
        features, src_tile, rel_type, timestamps, edge_tiles,
        rel_weight, attn_gain, w_qkv, w_out, cotangent,
    ):
        part, rel = aggregate(features, src_tile, rel_type, edge_tiles, rel_weight)
        layer_out, grad_qkv, grad_out, gain, grel = training_step(
            nf, nb, part, rel, timestamps, attn_gain, w_qkv, w_out, cotangent
        )
        return (
            layer_out,
            grad_qkv,
            grad_out,
            gain[0].astype(BF16),
            grel.reshape(NREL, rel.shape[2], D),
        )

    in_specs = (
        P("batch", "feat"),
        P("batch", None),
        P("batch", None),
        P(("batch", "feat")),
        P(),
        P(None, "feat", None),
        P(),
        P(),
        P(),
        P(("batch", "feat"), None),
    )
    out_specs = (P(("batch", "feat"), None), P(), P(), P(), P(None, "feat", None))
    return jax.shard_map(shards, mesh=mesh, in_specs=in_specs, out_specs=out_specs, check_vma=False)
```

```python
import functools

import jax
import jax.numpy as jnp
from jax import lax
from jax.experimental import pallas as pl
from jax.experimental.pallas import tpu as pltpu
from jax.sharding import PartitionSpec as P

D = 512
HEADS = 8
HEAD_DIM = 64
NREL = 4
SLOTS = 2
SBLK = 1024
EPS = 1e-06
STEP = 128
LAG = 6
F32 = jnp.float32
BF16 = jnp.bfloat16
MESH = pl.DeviceIdType.MESH
NT = (((1,), (1,)), ((), ()))
TN = (((0,), (0,)), ((), ()))
NN = (((1,), (0,)), ((), ()))


def mm(a, b, dims=NN):
    return lax.dot_general(a, b, dims, preferred_element_type=F32)


def remote(src, dst, send, recv, device):
    return pltpu.make_async_remote_copy(
        src_ref=src, dst_ref=dst, send_sem=send, recv_sem=recv, device_id=device, device_id_type=MESH
    )


def step_kernel(
    nf, nb, features, src, kind, edges, rel_w, times, gain, wqkv, wout, cot,
    out, qkv_out, w_out_out, gain_out, grel,
    feats, feats_sem, part, rel, grads, rs_sib, rs_stage, rs_recv, dt, gterm, g_sib, g_stage, g_recv,
    zl, zr, zs, gzl, gzr, gzs, gain_in, gain_z, proj, ctx, dproj,
    rs_s, rs_r, g_s, g_r, dt_s, dt_r, ag_s, ag_r, ga_s, ga_r, gz_s, gz_r,
    red_s, redl_r, redr_r, bl_s, br_s, bc_r,
):
    me = lax.axis_index("feat")
    z = lax.axis_index("batch")
    nc = nf // 2
    chip, core = me // 2, me % 2
    sib = me + 1 - 2 * core
    sibling = {"feat": sib}
    rows, cols = rel.shape[1], rel.shape[2]
    length = out.shape[0]
    quarters = cols // STEP
    chunks = NREL * quarters
    slab = D // nf

    def ahead(d):
        return 2 * ((chip + d) % nc) + core

    def behind(d):
        return 2 * ((chip + nc - d) % nc) + core

    feats_copy = pltpu.make_async_copy(features, feats, feats_sem)
    feats_copy.start()
    barrier = pltpu.get_barrier_semaphore()
    pl.semaphore_signal(barrier, inc=1, device_id=sibling, device_id_type=MESH)
    for d in range(1, nc):
        pl.semaphore_signal(barrier, inc=1, device_id={"feat": ahead(d)}, device_id_type=MESH)
    for d in range(1, nb):
        pl.semaphore_signal(barrier, inc=1, device_id={"batch": (z + d) % nb}, device_id_type=MESH)
    pl.semaphore_wait(barrier, nc + nb - 1)

    def rs_pair(src, half, send, recv):
        return remote(src.at[1 - core], half, send.at[0], recv.at[0], sibling)

    def rs_chip(stage, landed, send, recv, d):
        return remote(stage.at[(chip + d) % nc], landed.at[d], send.at[d], recv.at[d], {"feat": ahead(d)})

    def rs_mid(src, half, stage, landed, send, recv):
        rs_pair(src, half, send, recv).wait_recv()
        for d in range(1, nc):
            c = (chip + d) % nc
            stage[c] = (src[core, c].astype(F32) + half[c].astype(F32)).astype(BF16)
            rs_chip(stage, landed, send, recv, d).start()

    def rs_end(src, half, stage, landed, send, recv):
        value = src[core, chip].astype(F32) + half[chip].astype(F32)
        for d in range(1, nc):
            rs_chip(stage, landed, send, recv, d).wait_recv()
            value = value + landed[d].astype(F32)
        return value

    def rs_drain(src, half, stage, landed, send, recv):
        rs_pair(src, half, send, recv).wait_send()
        for d in range(1, nc):
            rs_chip(stage, landed, send, recv, d).wait_send()

    def ag_copy(buf, send, recv, d):
        device = sibling if d == 0 else {"feat": ahead(d)}
        return remote(buf.at[me], buf.at[me], send.at[d], recv.at[d], device)

    def ag_hand(buf, send, recv, d):
        slot = behind(d)
        return remote(buf.at[slot], buf.at[slot], send.at[nc - 1 + d], recv.at[nc - 1 + d], sibling)

    def ag_landed(buf, send, recv, slot, index):
        return remote(buf.at[slot], buf.at[slot], send.at[index], recv.at[index], sibling)

    def ag_start(*group):
        for d in list(range(1, nc)) + [0]:
            ag_copy(*group, d).start()

    def ag_mid(*group):
        for d in range(1, nc):
            ag_landed(*group, behind(d), d).wait_recv()
            ag_hand(*group, d).start()

    def ag_end(*group):
        ag_landed(*group, sib, 0).wait_recv()
        for d in range(1, nc):
            ag_landed(*group, behind(d) + 1 - 2 * core, nc - 1 + d).wait_recv()

    def ag_drain(*group):
        for d in range(nc):
            ag_copy(*group, d).wait_send()
        for d in range(1, nc):
            ag_hand(*group, d).wait_send()

    grad_rs = (gterm, g_sib, g_stage, g_recv, g_s, g_r)
    dt_ag = (dt, dt_s, dt_r)
    grad_ag = (grads, ag_s, ag_r)
    gain_ag = (gain_in, ga_s, ga_r)

    def project(half, c):
        b = 2 * c + half
        k0, k1 = kind[0, b], kind[1, b]
        p0 = mm(edges[k0], feats[src[0, b]])
        p1 = mm(edges[k1], feats[src[1, b]])
        same = (k0 == k1).astype(F32)
        first = (p0 + same * p1).astype(BF16)
        second = ((1.0 - same) * p1).astype(BF16)
        here = pl.ds(pl.multiple_of(b * length, length), length)
        for relation in range(NREL):
            is_first = (k0 == relation).astype(F32)
            is_second = (k1 == relation).astype(F32)
            rel[relation, here, :] = (is_first * first.astype(F32) + is_second * second.astype(F32)).astype(BF16)
        part[half, c] = (mm(first, rel_w[k0]) + mm(second, rel_w[k1])).astype(BF16)

    def to_sibling(c):
        return remote(part.at[1 - core, c], rs_sib.at[c], rs_s.at[nc + c], rs_r.at[nc + c], sibling)

    def to_chip(d):
        return rs_chip(rs_stage, rs_recv, rs_s, rs_r, d)

    def other_half(c, carry):
        project(1 - core, c)
        to_sibling(c).start()
        return carry

    def own_half(d, carry):
        c = (chip + d) % nc
        project(core, c)
        to_sibling(c).wait_recv()
        rs_stage[c] = (part[core, c].astype(F32) + rs_sib[c].astype(F32)).astype(BF16)
        to_chip(d).start()
        return carry

    feats_copy.wait()
    lax.fori_loop(0, nc, other_half, 0)
    lax.fori_loop(1, nc, own_half, 0)
    project(core, chip)
    d_ctx = mm(cot[...], wout[...], NT).astype(BF16)
    row_times = jnp.broadcast_to(times[...], (length, length))
    allowed = row_times <= row_times.T
    to_sibling(chip).wait_recv()
    total = part[core, chip].astype(F32) + rs_sib[chip].astype(F32)
    for d in range(1, nc):
        to_chip(d).wait_recv()
        total = total + rs_recv[d].astype(F32)

    sigma = 1.0 / (1.0 + jnp.exp(-total))
    tokens = (total * sigma).astype(BF16).astype(F32)
    scale = lax.rsqrt(jnp.mean(tokens * tokens, axis=-1, keepdims=True) + EPS)
    normed = (tokens * scale * gain[...]).astype(BF16)
    proj[...] = mm(normed, wqkv[...]).astype(BF16)
    heads = range(HEADS)
    spans = [(h * HEAD_DIM, (h + 1) * HEAD_DIM) for h in heads]
    q = [proj[:, a:b] for a, b in spans]
    k = [proj[:, D + a : D + b] for a, b in spans]
    v = [proj[:, 2 * D + a : 2 * D + b] for a, b in spans]
    dc = [d_ctx[:, a:b] for a, b in spans]
    scores = [mm(q[h], k[h], NT) for h in heads]
    dw = [mm(dc[h], v[h], NT) for h in heads]
    p, ds = [], []
    for h in heads:
        masked = jnp.where(allowed, scores[h] * (HEAD_DIM**-0.5), -1e30)
        e = jnp.exp(masked - jnp.max(masked, axis=-1, keepdims=True))
        ph = e / jnp.sum(e, axis=-1, keepdims=True)
        dwh = dw[h].astype(BF16).astype(F32)
        dsh = ph * (dwh - jnp.sum(dwh * ph, axis=-1, keepdims=True))
        p.append(ph.astype(BF16))
        ds.append((jnp.where(allowed, dsh, 0.0) * (HEAD_DIM**-0.5)).astype(BF16))
    for h, (a, b) in enumerate(spans):
        dproj[:, a:b] = mm(ds[h], k[h]).astype(BF16)
        dproj[:, D + a : D + b] = mm(ds[h], q[h], TN).astype(BF16)
        dproj[:, 2 * D + a : 2 * D + b] = mm(p[h], dc[h], TN).astype(BF16)
    d_normed = mm(dproj[...], wqkv[...], NT).astype(BF16).astype(F32)
    u = d_normed * gain[...]
    inner = jnp.sum(u * tokens, axis=-1, keepdims=True)
    d_tokens = cot[...].astype(F32) + u * scale - tokens * (scale * scale * scale * inner * (1.0 / D))
    d_hidden = d_tokens.astype(BF16).astype(F32)
    dt[me] = (d_hidden * (sigma * (1.0 + total * (1.0 - sigma)))).astype(BF16)
    ag_start(*dt_ag)
    gain_term = jnp.sum(d_normed * (tokens * scale), axis=0, keepdims=True)
    gain_in[me] = jnp.broadcast_to(gain_term, (8, D))
    for h, (a, b) in enumerate(spans):
        ctx[:, a:b] = mm(p[h], v[h]).astype(BF16)
    out[...] = (tokens + mm(ctx[...], wout[...])).astype(BF16)
    g_qkv = mm(normed, dproj[...], TN).astype(BF16)
    for j in range(nf):
        gterm[j % 2, j // 2, :, : 3 * D] = g_qkv[j * slab : (j + 1) * slab]
    g_out = mm(ctx[...], cot[...], TN).astype(BF16)
    for j in range(nf):
        gterm[j % 2, j // 2, :, 3 * D :] = g_out[j * slab : (j + 1) * slab]
    rs_pair(gterm, g_sib, g_s, g_r).start()
    ag_start(*gain_ag)
    ag_mid(*dt_ag)
    rs_mid(*grad_rs)
    ag_end(*dt_ag)

    owner = nb // 2 - 1 + core
    up, down = {"batch": lax.rem(z + 1, nb)}, {"batch": lax.rem(z + nb - 1, nb)}

    def hop_up(stage, landed, i):
        return remote(stage, landed, red_s.at[i], redl_r.at[i], up)

    def hop_down(stage, landed, i):
        return remote(stage, landed, red_s.at[i], redr_r.at[i], down)

    def give_up(result, i):
        return remote(result, result, br_s.at[i], bc_r.at[i], up)

    def give_down(result, i):
        return remote(result, result, bl_s.at[i], bc_r.at[i], down)

    def reduce(own, low, high, stage, result, i):
        @pl.when(z == 0)
        def _():
            stage[...] = own.astype(BF16)
            hop_up(stage, low, i).start()

        @pl.when((z > 0) & (z < owner))
        def _():
            hop_up(stage, low, i).wait_recv()
            stage[...] = (own + low[...].astype(F32)).astype(BF16)
            hop_up(stage, low, i).start()

        @pl.when(z == nb - 1)
        def _():
            stage[...] = own.astype(BF16)
            hop_down(stage, high, i).start()

        @pl.when((z > owner) & (z < nb - 1))
        def _():
            hop_down(stage, high, i).wait_recv()
            stage[...] = (own + high[...].astype(F32)).astype(BF16)
            hop_down(stage, high, i).start()

        @pl.when(z == owner)
        def _():
            hop_up(stage, low, i).wait_recv()
            hop_down(stage, high, i).wait_recv()
            result[...] = (own + low[...].astype(F32) + high[...].astype(F32)).astype(BF16)
            give_up(result, i).start()
            give_down(result, i).start()

    edge = (z == 0) | (z == nb - 1)

    def spread(result, i):
        @pl.when((z > 0) & (z < owner))
        def _():
            give_down(result, i).wait_recv()
            give_down(result, i).start()

        @pl.when((z > owner) & (z < nb - 1))
        def _():
            give_up(result, i).wait_recv()
            give_up(result, i).start()

    def settle(result, i):
        @pl.when(edge)
        def _():
            give_up(result, i).wait_recv()

    def drain(low, stage, result, i):
        @pl.when(z != owner)
        def _():
            hop_up(stage, low, i).wait_send()

        @pl.when((z <= owner) & (z > 0))
        def _():
            give_down(result, i).wait_send()

        @pl.when((z >= owner) & (z < nb - 1))
        def _():
            give_up(result, i).wait_send()

    def chunk_out(i):
        return grel.at[pl.ds(pl.multiple_of(i * STEP, STEP), STEP)]

    def reduce_rel(i):
        left = rel[i // quarters, :, pl.ds(pl.multiple_of((i % quarters) * STEP, STEP), STEP)]
        own = mm(left, dt[...].reshape(rows, D), TN)
        reduce(own, zl.at[i], zr.at[i], zs.at[i], chunk_out(i), i)

    def both(i, carry):
        reduce_rel(i)
        spread(chunk_out(i - lag), i - lag)
        return carry

    def only_reduce(i, carry):
        reduce_rel(i)
        return carry

    def only_spread(i, carry):
        spread(chunk_out(i), i)
        return carry

    def only_settle(i, carry):
        settle(chunk_out(i), i)
        return carry

    lag = min(LAG, chunks // 2)
    turn = lag
    mine = grads.at[me]
    lax.fori_loop(0, lag, only_reduce, 0)
    ag_mid(*gain_ag)
    ag_end(*gain_ag)
    group_gain = gain_in[0]
    for j in range(1, nf):
        group_gain = group_gain + gain_in[j]
    gain_z[z] = group_gain

    def gain_copy(d):
        return remote(gain_z.at[z], gain_z.at[z], gz_s.at[d], gz_r.at[d], {"batch": (z + d) % nb})

    def gain_landed(d):
        slot = (z + nb - d) % nb
        return remote(gain_z.at[slot], gain_z.at[slot], gz_s.at[d], gz_r.at[d], {"batch": slot})

    for d in range(1, nb):
        gain_copy(d).start()
    reduce(rs_end(*grad_rs), gzl, gzr, gzs, mine, chunks)
    lax.fori_loop(turn, turn + lag, both, 0)
    spread(mine, chunks)

    @pl.when(jnp.logical_not(edge))
    def _():
        ag_start(*grad_ag)

    lax.fori_loop(turn + lag, chunks, both, 0)
    settle(mine, chunks)

    @pl.when(edge)
    def _():
        ag_start(*grad_ag)

    ag_mid(*grad_ag)
    lax.fori_loop(chunks - lag, chunks, only_spread, 0)
    lax.fori_loop(0, chunks, only_settle, 0)
    for d in range(1, nb):
        gain_landed(d).wait_recv()
    whole_gain = gain_z[0]
    for j in range(1, nb):
        whole_gain = whole_gain + gain_z[j]
    gain_out[...] = whole_gain
    ag_end(*grad_ag)
    for j in range(nf):
        qkv_out[j * slab : (j + 1) * slab] = grads[j, :, : 3 * D]
        w_out_out[j * slab : (j + 1) * slab] = grads[j, :, 3 * D :]

    def drain_rel(i, carry):
        drain(zl.at[i], zs.at[i], chunk_out(i), i)
        return carry

    lax.fori_loop(0, chunks, drain_rel, 0)
    drain(gzl, gzs, mine, chunks)
    for d in range(1, nb):
        gain_copy(d).wait_send()
    for c in range(nc):
        to_sibling(c).wait_send()
    for d in range(1, nc):
        to_chip(d).wait_send()
    rs_drain(*grad_rs)
    ag_drain(*dt_ag)
    ag_drain(*gain_ag)
    ag_drain(*grad_ag)


def training_step(
    nf, nb, features, src_tile, rel_type, edge_tiles, rel_weight, timestamps, gain, w_qkv, w_out, cotangent
):
    nc = nf // 2
    length = timestamps.shape[0]
    cols = features.shape[1]
    slab = D // nf
    chunks = NREL * cols // STEP
    vmem = pl.BlockSpec(memory_space=pltpu.VMEM)
    blocks = pltpu.VMEM((nc, length, D), BF16)
    slabs = pltpu.VMEM((nc, slab, 4 * D), BF16)
    pieces = pltpu.VMEM((chunks, STEP, D), BF16)
    piece = pltpu.VMEM((slab, 4 * D), BF16)
    dma = pltpu.SemaphoreType.DMA
    return pl.pallas_call(
        functools.partial(step_kernel, nf, nb),
        out_shape=[
            jax.ShapeDtypeStruct((length, D), BF16),
            jax.ShapeDtypeStruct((D, 3 * D), BF16),
            jax.ShapeDtypeStruct((D, D), BF16),
            jax.ShapeDtypeStruct((8, D), F32),
            jax.ShapeDtypeStruct((NREL * cols, D), BF16),
        ],
        in_specs=[pl.BlockSpec(memory_space=pl.ANY)]
        + [pl.BlockSpec(memory_space=pltpu.SMEM)] * 2
        + [vmem] * 7,
        out_specs=[vmem] * 5,
        scratch_shapes=[
            pltpu.VMEM((features.shape[0] // SBLK, SBLK, cols), BF16),
            dma(()),
            pltpu.VMEM((2, nc, length, D), BF16),
            pltpu.VMEM((NREL, nf * length, cols), BF16),
            pltpu.VMEM((nf, slab, 4 * D), BF16),
            blocks, blocks, blocks,
            pltpu.VMEM((nf, length, D), BF16),
            pltpu.VMEM((2, nc, slab, 4 * D), BF16),
            slabs, slabs, slabs,
            pieces, pieces, pieces,
            piece, piece, piece,
            pltpu.VMEM((nf, 8, D), F32),
            pltpu.VMEM((nb, 8, D), F32),
            pltpu.VMEM((length, 3 * D), BF16),
            pltpu.VMEM((length, D), BF16),
            pltpu.VMEM((length, 3 * D), BF16),
        ]
        + [dma((2 * nc,))] * 2
        + [dma((nc,))] * 2
        + [dma((2 * nc - 1,))] * 6
        + [dma((nb,))] * 2
        + [dma((chunks + 1,))] * 6,
        compiler_params=pltpu.CompilerParams(
            collective_id=0, has_side_effects=True, vmem_limit_bytes=60 * 2**20
        ),
        name="training_step",
    )(
        features.reshape(-1, SBLK, cols), src_tile.T, rel_type.T, edge_tiles, rel_weight,
        timestamps.reshape(1, -1), gain.reshape(1, -1), w_qkv, w_out, cotangent,
    )


def hand_out_kernel(count, *refs):
    arrays, gain = refs[:count], refs[count]
    results, gain_out, sems = refs[count + 1 : -2], refs[-2], refs[-1]
    copies = []
    for array, result in zip(arrays, results):
        piece = min(512, array.shape[0])
        for start in range(0, array.shape[0], piece):
            span = pl.ds(start, piece)
            copies.append((array.at[span], result.at[span]))
    copies = [pltpu.make_async_copy(a, b, sems.at[i]) for i, (a, b) in enumerate(copies)]
    for copy in copies:
        copy.start()
    gain_out[...] = gain[0].astype(BF16)
    for copy in copies:
        copy.wait()


def hand_out(arrays, gain):
    anywhere = pl.BlockSpec(memory_space=pl.ANY)
    vmem = pl.BlockSpec(memory_space=pltpu.VMEM)
    pieces = sum(max(1, array.shape[0] // 512) for array in arrays)
    return pl.pallas_call(
        functools.partial(hand_out_kernel, len(arrays)),
        out_shape=[jax.ShapeDtypeStruct(a.shape, a.dtype) for a in arrays]
        + [jax.ShapeDtypeStruct((D,), BF16)],
        in_specs=[anywhere] * len(arrays) + [vmem],
        out_specs=[anywhere] * len(arrays) + [vmem],
        scratch_shapes=[pltpu.SemaphoreType.DMA((pieces,))],
        compiler_params=pltpu.CompilerParams(vmem_limit_bytes=60 * 2**20),
        name="hand_out",
    )(*arrays, gain)


def solution(mesh):
    nf, nb = mesh.shape["feat"], mesh.shape["batch"]

    def shards(
        features, src_tile, rel_type, timestamps, edge_tiles,
        rel_weight, attn_gain, w_qkv, w_out, cotangent,
    ):
        *results, gain, grel = training_step(
            nf, nb, features, src_tile, rel_type, edge_tiles, rel_weight,
            timestamps, attn_gain, w_qkv, w_out, cotangent,
        )
        layer_out, grad_qkv, grad_out, grel, gain = hand_out((*results, grel), gain)
        return layer_out, grad_qkv, grad_out, gain, grel.reshape(NREL, features.shape[1], D)

    in_specs = (
        P("batch", "feat"),
        P("batch", None),
        P("batch", None),
        P(("batch", "feat")),
        P(),
        P(None, "feat", None),
        P(),
        P(),
        P(),
        P(("batch", "feat"), None),
    )
    out_specs = (P(("batch", "feat"), None), P(), P(), P(), P(None, "feat", None))
    return jax.shard_map(shards, mesh=mesh, in_specs=in_specs, out_specs=out_specs, check_vma=False)
```

```python
import functools

import jax
import jax.numpy as jnp
from jax import lax
from jax.experimental import pallas as pl
from jax.experimental.pallas import tpu as pltpu
from jax.sharding import PartitionSpec as P

D = 512
HEADS = 8
HEAD_DIM = 64
NREL = 4
SLOTS = 2
SBLK = 1024
EPS = 1e-06
STEP = 128
LAG = 6
PIECE = 64
F32 = jnp.float32
BF16 = jnp.bfloat16
MESH = pl.DeviceIdType.MESH
NT = (((1,), (1,)), ((), ()))
TN = (((0,), (0,)), ((), ()))
NN = (((1,), (0,)), ((), ()))


def mm(a, b, dims=NN):
    return lax.dot_general(a, b, dims, preferred_element_type=F32)


def remote(src, dst, send, recv, device):
    return pltpu.make_async_remote_copy(
        src_ref=src, dst_ref=dst, send_sem=send, recv_sem=recv, device_id=device, device_id_type=MESH
    )


def step_kernel(
    nf, nb, features, src, kind, edges, rel_w, times, gain, wqkv, wout, cot,
    out, qkv_out, w_out_out, gain_out, grel,
    feats, feats_sem, part, rel, grads, rs_sib, rs_stage, rs_recv, dt, gterm, g_sib, g_stage, g_recv,
    zl, zr, zs, gzl, gzr, gzs, gain_in, gain_z, proj, ctx, dproj,
    rs_s, rs_r, g_s, g_r, dt_s, dt_r, ag_s, ag_r, ga_s, ga_r, gz_s, gz_r,
    red_s, redl_r, redr_r, bl_s, br_s, bc_r,
):
    me = lax.axis_index("feat")
    z = lax.axis_index("batch")
    nc = nf // 2
    chip, core = me // 2, me % 2
    sib = me + 1 - 2 * core
    sibling = {"feat": sib}
    rows, cols = rel.shape[1], rel.shape[2]
    length = out.shape[0]
    quarters = cols // STEP
    chunks = NREL * quarters
    slab = D // nf
    split = STEP // PIECE
    pieces = split * chunks
    lag = min(LAG, chunks // 2)

    def ahead(d):
        return 2 * ((chip + d) % nc) + core

    def behind(d):
        return 2 * ((chip + nc - d) % nc) + core

    feats_copy = pltpu.make_async_copy(features, feats, feats_sem)
    feats_copy.start()
    barrier = pltpu.get_barrier_semaphore()
    pl.semaphore_signal(barrier, inc=1, device_id=sibling, device_id_type=MESH)
    for d in range(1, nc):
        pl.semaphore_signal(barrier, inc=1, device_id={"feat": ahead(d)}, device_id_type=MESH)
    for d in range(1, nb):
        pl.semaphore_signal(barrier, inc=1, device_id={"batch": (z + d) % nb}, device_id_type=MESH)
    pl.semaphore_wait(barrier, nc + nb - 1)

    def rs_pair(src, half, send, recv):
        return remote(src.at[1 - core], half, send.at[0], recv.at[0], sibling)

    def rs_chip(stage, landed, send, recv, d):
        return remote(stage.at[(chip + d) % nc], landed.at[d], send.at[d], recv.at[d], {"feat": ahead(d)})

    def rs_mid(src, half, stage, landed, send, recv):
        rs_pair(src, half, send, recv).wait_recv()
        for d in range(1, nc):
            c = (chip + d) % nc
            stage[c] = (src[core, c].astype(F32) + half[c].astype(F32)).astype(BF16)
            rs_chip(stage, landed, send, recv, d).start()

    def rs_end(src, half, stage, landed, send, recv):
        value = src[core, chip].astype(F32) + half[chip].astype(F32)
        for d in range(1, nc):
            rs_chip(stage, landed, send, recv, d).wait_recv()
            value = value + landed[d].astype(F32)
        return value

    def rs_drain(src, half, stage, landed, send, recv):
        rs_pair(src, half, send, recv).wait_send()
        for d in range(1, nc):
            rs_chip(stage, landed, send, recv, d).wait_send()

    def ag_copy(buf, send, recv, d):
        device = sibling if d == 0 else {"feat": ahead(d)}
        return remote(buf.at[me], buf.at[me], send.at[d], recv.at[d], device)

    def ag_hand(buf, send, recv, d):
        slot = behind(d)
        return remote(buf.at[slot], buf.at[slot], send.at[nc - 1 + d], recv.at[nc - 1 + d], sibling)

    def ag_landed(buf, send, recv, slot, index):
        return remote(buf.at[slot], buf.at[slot], send.at[index], recv.at[index], sibling)

    def ag_start(*group):
        for d in list(range(1, nc)) + [0]:
            ag_copy(*group, d).start()

    def ag_mid(*group):
        for d in range(1, nc):
            ag_landed(*group, behind(d), d).wait_recv()
            ag_hand(*group, d).start()

    def ag_end(*group):
        ag_landed(*group, sib, 0).wait_recv()
        for d in range(1, nc):
            ag_landed(*group, behind(d) + 1 - 2 * core, nc - 1 + d).wait_recv()

    def ag_drain(*group):
        for d in range(nc):
            ag_copy(*group, d).wait_send()
        for d in range(1, nc):
            ag_hand(*group, d).wait_send()

    grad_rs = (gterm, g_sib, g_stage, g_recv, g_s, g_r)
    dt_ag = (dt, dt_s, dt_r)
    grad_ag = (grads, ag_s, ag_r)
    gain_ag = (gain_in, ga_s, ga_r)

    def project(half, c):
        b = 2 * c + half
        k0, k1 = kind[0, b], kind[1, b]
        p0 = mm(edges[k0], feats[src[0, b]])
        p1 = mm(edges[k1], feats[src[1, b]])
        same = (k0 == k1).astype(F32)
        first = (p0 + same * p1).astype(BF16)
        second = ((1.0 - same) * p1).astype(BF16)
        here = pl.ds(pl.multiple_of(b * length, length), length)
        for relation in range(NREL):
            is_first = (k0 == relation).astype(F32)
            is_second = (k1 == relation).astype(F32)
            rel[relation, here, :] = (is_first * first.astype(F32) + is_second * second.astype(F32)).astype(BF16)
        part[half, c] = (mm(first, rel_w[k0]) + mm(second, rel_w[k1])).astype(BF16)

    def to_sibling(c):
        return remote(part.at[1 - core, c], rs_sib.at[c], rs_s.at[nc + c], rs_r.at[nc + c], sibling)

    def to_chip(d):
        return rs_chip(rs_stage, rs_recv, rs_s, rs_r, d)

    def other_half(c, carry):
        project(1 - core, c)
        to_sibling(c).start()
        return carry

    def own_half(d, carry):
        c = (chip + d) % nc
        project(core, c)
        to_sibling(c).wait_recv()
        rs_stage[c] = (part[core, c].astype(F32) + rs_sib[c].astype(F32)).astype(BF16)
        to_chip(d).start()
        return carry

    feats_copy.wait()
    lax.fori_loop(0, nc, other_half, 0)
    lax.fori_loop(1, nc, own_half, 0)
    project(core, chip)
    d_ctx = mm(cot[...], wout[...], NT).astype(BF16)
    row_times = jnp.broadcast_to(times[...], (length, length))
    allowed = row_times <= row_times.T
    to_sibling(chip).wait_recv()
    total = part[core, chip].astype(F32) + rs_sib[chip].astype(F32)
    for d in range(1, nc):
        to_chip(d).wait_recv()
        total = total + rs_recv[d].astype(F32)

    sigma = 1.0 / (1.0 + jnp.exp(-total))
    tokens = (total * sigma).astype(BF16).astype(F32)
    scale = lax.rsqrt(jnp.mean(tokens * tokens, axis=-1, keepdims=True) + EPS)
    normed = (tokens * scale * gain[...]).astype(BF16)
    proj[...] = mm(normed, wqkv[...]).astype(BF16)
    heads = range(HEADS)
    spans = [(h * HEAD_DIM, (h + 1) * HEAD_DIM) for h in heads]
    q = [proj[:, a:b] for a, b in spans]
    k = [proj[:, D + a : D + b] for a, b in spans]
    v = [proj[:, 2 * D + a : 2 * D + b] for a, b in spans]
    dc = [d_ctx[:, a:b] for a, b in spans]
    scores = [mm(q[h], k[h], NT) for h in heads]
    dw = [mm(dc[h], v[h], NT) for h in heads]
    p, ds = [], []
    for h in heads:
        masked = jnp.where(allowed, scores[h] * (HEAD_DIM**-0.5), -1e30)
        e = jnp.exp(masked - jnp.max(masked, axis=-1, keepdims=True))
        ph = e / jnp.sum(e, axis=-1, keepdims=True)
        dwh = dw[h].astype(BF16).astype(F32)
        dsh = ph * (dwh - jnp.sum(dwh * ph, axis=-1, keepdims=True))
        p.append(ph.astype(BF16))
        ds.append((jnp.where(allowed, dsh, 0.0) * (HEAD_DIM**-0.5)).astype(BF16))
    for h, (a, b) in enumerate(spans):
        dproj[:, a:b] = mm(ds[h], k[h]).astype(BF16)
        dproj[:, D + a : D + b] = mm(ds[h], q[h], TN).astype(BF16)
        dproj[:, 2 * D + a : 2 * D + b] = mm(p[h], dc[h], TN).astype(BF16)
    d_normed = mm(dproj[...], wqkv[...], NT).astype(BF16).astype(F32)
    u = d_normed * gain[...]
    inner = jnp.sum(u * tokens, axis=-1, keepdims=True)
    d_tokens = cot[...].astype(F32) + u * scale - tokens * (scale * scale * scale * inner * (1.0 / D))
    d_hidden = d_tokens.astype(BF16).astype(F32)
    dt[me] = (d_hidden * (sigma * (1.0 + total * (1.0 - sigma)))).astype(BF16)
    ag_start(*dt_ag)
    gain_term = jnp.sum(d_normed * (tokens * scale), axis=0, keepdims=True)
    gain_in[me] = jnp.broadcast_to(gain_term, (8, D))
    for h, (a, b) in enumerate(spans):
        ctx[:, a:b] = mm(p[h], v[h]).astype(BF16)
    out[...] = (tokens + mm(ctx[...], wout[...])).astype(BF16)
    g_qkv = mm(normed, dproj[...], TN).astype(BF16)
    for j in range(nf):
        gterm[j % 2, j // 2, :, : 3 * D] = g_qkv[j * slab : (j + 1) * slab]
    g_out = mm(ctx[...], cot[...], TN).astype(BF16)
    for j in range(nf):
        gterm[j % 2, j // 2, :, 3 * D :] = g_out[j * slab : (j + 1) * slab]
    rs_pair(gterm, g_sib, g_s, g_r).start()
    ag_start(*gain_ag)
    ag_mid(*dt_ag)
    rs_mid(*grad_rs)
    ag_end(*dt_ag)

    owner = nb // 2 - 1 + core
    up, down = {"batch": lax.rem(z + 1, nb)}, {"batch": lax.rem(z + nb - 1, nb)}

    def hop_up(stage, landed, i):
        return remote(stage, landed, red_s.at[i], redl_r.at[i], up)

    def hop_down(stage, landed, i):
        return remote(stage, landed, red_s.at[i], redr_r.at[i], down)

    def give_up(result, i):
        return remote(result, result, br_s.at[i], bc_r.at[i], up)

    def give_down(result, i):
        return remote(result, result, bl_s.at[i], bc_r.at[i], down)

    def reduce(own, low, high, stage, result, i):
        @pl.when(z == 0)
        def _():
            stage[...] = own.astype(BF16)
            hop_up(stage, low, i).start()

        @pl.when((z > 0) & (z < owner))
        def _():
            hop_up(stage, low, i).wait_recv()
            stage[...] = (own + low[...].astype(F32)).astype(BF16)
            hop_up(stage, low, i).start()

        @pl.when(z == nb - 1)
        def _():
            stage[...] = own.astype(BF16)
            hop_down(stage, high, i).start()

        @pl.when((z > owner) & (z < nb - 1))
        def _():
            hop_down(stage, high, i).wait_recv()
            stage[...] = (own + high[...].astype(F32)).astype(BF16)
            hop_down(stage, high, i).start()

        @pl.when(z == owner)
        def _():
            hop_up(stage, low, i).wait_recv()
            hop_down(stage, high, i).wait_recv()
            result[...] = (own + low[...].astype(F32) + high[...].astype(F32)).astype(BF16)
            give_up(result, i).start()
            give_down(result, i).start()

    edge = (z == 0) | (z == nb - 1)

    def spread(result, i):
        @pl.when((z > 0) & (z < owner))
        def _():
            give_down(result, i).wait_recv()
            give_down(result, i).start()

        @pl.when((z > owner) & (z < nb - 1))
        def _():
            give_up(result, i).wait_recv()
            give_up(result, i).start()

    def settle(result, i):
        @pl.when(edge)
        def _():
            give_up(result, i).wait_recv()

    def drain(low, stage, result, i):
        @pl.when(z != owner)
        def _():
            hop_up(stage, low, i).wait_send()

        @pl.when((z <= owner) & (z > 0))
        def _():
            give_down(result, i).wait_send()

        @pl.when((z >= owner) & (z < nb - 1))
        def _():
            give_up(result, i).wait_send()

    def chunk_out(i):
        return grel.at[pl.ds(pl.multiple_of(i * PIECE, PIECE), PIECE)]

    def reduce_rel(i, behind_too):
        left = rel[i // quarters, :, pl.ds(pl.multiple_of((i % quarters) * STEP, STEP), STEP)]
        own = mm(left, dt[...].reshape(rows, D), TN)
        for half in range(split):
            j = split * i + half
            mine_now = own[half * PIECE : (half + 1) * PIECE]
            reduce(mine_now, zl.at[j], zr.at[j], zs.at[j], chunk_out(j), j)
            if behind_too:
                spread(chunk_out(j - split * lag), j - split * lag)

    def both(i, carry):
        reduce_rel(i, True)
        return carry

    def only_reduce(i, carry):
        reduce_rel(i, False)
        return carry

    def only_spread(i, carry):
        spread(chunk_out(i), i)
        return carry

    def only_settle(i, carry):
        settle(chunk_out(i), i)
        return carry

    turn = lag
    mine = grads.at[me]
    lax.fori_loop(0, lag, only_reduce, 0)
    ag_mid(*gain_ag)
    ag_end(*gain_ag)
    group_gain = gain_in[0]
    for j in range(1, nf):
        group_gain = group_gain + gain_in[j]
    gain_z[z] = group_gain

    def gain_copy(d):
        return remote(gain_z.at[z], gain_z.at[z], gz_s.at[d], gz_r.at[d], {"batch": (z + d) % nb})

    def gain_landed(d):
        slot = (z + nb - d) % nb
        return remote(gain_z.at[slot], gain_z.at[slot], gz_s.at[d], gz_r.at[d], {"batch": slot})

    for d in range(1, nb):
        gain_copy(d).start()
    reduce(rs_end(*grad_rs), gzl, gzr, gzs, mine, pieces)
    lax.fori_loop(turn, turn + lag, both, 0)
    spread(mine, pieces)

    @pl.when(jnp.logical_not(edge))
    def _():
        ag_start(*grad_ag)

    lax.fori_loop(turn + lag, chunks, both, 0)
    settle(mine, pieces)

    @pl.when(edge)
    def _():
        ag_start(*grad_ag)

    lax.fori_loop(pieces - split * lag, pieces, only_spread, 0)
    ag_mid(*grad_ag)
    for d in range(1, nb):
        gain_landed(d).wait_recv()
    whole_gain = gain_z[0]
    for j in range(1, nb):
        whole_gain = whole_gain + gain_z[j]
    gain_out[...] = whole_gain
    ag_end(*grad_ag)
    for j in range(nf):
        qkv_out[j * slab : (j + 1) * slab] = grads[j, :, : 3 * D]
        w_out_out[j * slab : (j + 1) * slab] = grads[j, :, 3 * D :]
    lax.fori_loop(0, pieces, only_settle, 0)

    def drain_rel(i, carry):
        drain(zl.at[i], zs.at[i], chunk_out(i), i)
        return carry

    lax.fori_loop(0, pieces, drain_rel, 0)
    drain(gzl, gzs, mine, pieces)
    for d in range(1, nb):
        gain_copy(d).wait_send()
    for c in range(nc):
        to_sibling(c).wait_send()
    for d in range(1, nc):
        to_chip(d).wait_send()
    rs_drain(*grad_rs)
    ag_drain(*dt_ag)
    ag_drain(*gain_ag)
    ag_drain(*grad_ag)


def training_step(
    nf, nb, features, src_tile, rel_type, edge_tiles, rel_weight, timestamps, gain, w_qkv, w_out, cotangent
):
    nc = nf // 2
    length = timestamps.shape[0]
    cols = features.shape[1]
    slab = D // nf
    pieces = NREL * cols // PIECE
    vmem = pl.BlockSpec(memory_space=pltpu.VMEM)
    blocks = pltpu.VMEM((nc, length, D), BF16)
    slabs = pltpu.VMEM((nc, slab, 4 * D), BF16)
    lines = pltpu.VMEM((pieces, PIECE, D), BF16)
    piece = pltpu.VMEM((slab, 4 * D), BF16)
    dma = pltpu.SemaphoreType.DMA
    return pl.pallas_call(
        functools.partial(step_kernel, nf, nb),
        out_shape=[
            jax.ShapeDtypeStruct((length, D), BF16),
            jax.ShapeDtypeStruct((D, 3 * D), BF16),
            jax.ShapeDtypeStruct((D, D), BF16),
            jax.ShapeDtypeStruct((8, D), F32),
            jax.ShapeDtypeStruct((NREL * cols, D), BF16),
        ],
        in_specs=[pl.BlockSpec(memory_space=pl.ANY)]
        + [pl.BlockSpec(memory_space=pltpu.SMEM)] * 2
        + [vmem] * 7,
        out_specs=[vmem] * 5,
        scratch_shapes=[
            pltpu.VMEM((features.shape[0] // SBLK, SBLK, cols), BF16),
            dma(()),
            pltpu.VMEM((2, nc, length, D), BF16),
            pltpu.VMEM((NREL, nf * length, cols), BF16),
            pltpu.VMEM((nf, slab, 4 * D), BF16),
            blocks, blocks, blocks,
            pltpu.VMEM((nf, length, D), BF16),
            pltpu.VMEM((2, nc, slab, 4 * D), BF16),
            slabs, slabs, slabs,
            lines, lines, lines,
            piece, piece, piece,
            pltpu.VMEM((nf, 8, D), F32),
            pltpu.VMEM((nb, 8, D), F32),
            pltpu.VMEM((length, 3 * D), BF16),
            pltpu.VMEM((length, D), BF16),
            pltpu.VMEM((length, 3 * D), BF16),
        ]
        + [dma((2 * nc,))] * 2
        + [dma((nc,))] * 2
        + [dma((2 * nc - 1,))] * 6
        + [dma((nb,))] * 2
        + [dma((pieces + 1,))] * 6,
        compiler_params=pltpu.CompilerParams(
            collective_id=0, has_side_effects=True, vmem_limit_bytes=60 * 2**20
        ),
        name="training_step",
    )(
        features.reshape(-1, SBLK, cols), src_tile.T, rel_type.T, edge_tiles, rel_weight,
        timestamps.reshape(1, -1), gain.reshape(1, -1), w_qkv, w_out, cotangent,
    )


def hand_out_kernel(*refs):
    half = len(refs) // 2
    for array, result in zip(refs[: half - 1], refs[half:-1]):
        result[...] = array[...]
    refs[-1][...] = refs[half - 1][0].astype(BF16)


def hand_out(arrays, gain):
    steps = 4
    specs = [pl.BlockSpec((a.shape[0] // steps, a.shape[1]), lambda i: (i, 0)) for a in arrays]
    return pl.pallas_call(
        hand_out_kernel,
        grid=(steps,),
        out_shape=[jax.ShapeDtypeStruct(a.shape, a.dtype) for a in arrays]
        + [jax.ShapeDtypeStruct((D,), BF16)],
        in_specs=specs + [pl.BlockSpec(gain.shape, lambda i: (0, 0))],
        out_specs=specs + [pl.BlockSpec((D,), lambda i: (0,))],
        compiler_params=pltpu.CompilerParams(vmem_limit_bytes=60 * 2**20),
        name="hand_out",
    )(*arrays, gain)


def solution(mesh):
    nf, nb = mesh.shape["feat"], mesh.shape["batch"]

    def shards(
        features, src_tile, rel_type, timestamps, edge_tiles,
        rel_weight, attn_gain, w_qkv, w_out, cotangent,
    ):
        *results, gain, grel = training_step(
            nf, nb, features, src_tile, rel_type, edge_tiles, rel_weight,
            timestamps, attn_gain, w_qkv, w_out, cotangent,
        )
        layer_out, grad_qkv, grad_out, grel, gain = hand_out((*results, grel), gain)
        return layer_out, grad_qkv, grad_out, gain, grel.reshape(NREL, features.shape[1], D)

    in_specs = (
        P("batch", "feat"),
        P("batch", None),
        P("batch", None),
        P(("batch", "feat")),
        P(),
        P(None, "feat", None),
        P(),
        P(),
        P(),
        P(("batch", "feat"), None),
    )
    out_specs = (P(("batch", "feat"), None), P(), P(), P(), P(None, "feat", None))
    return jax.shard_map(shards, mesh=mesh, in_specs=in_specs, out_specs=out_specs, check_vma=False)
```
